32 devices in a mesh: groups: 2 (over x), seq: 16 (over z, y, core).
Axes of the slice: x: 2, y: 2, z: 4, core: 2. Of those that a mesh axis runs over, the one named last changes fastest.
Arguments:
- tokens: bfloat16 [8192, 256], P(('groups', 'seq')), parts along dimension 0, may hold values from -6 to 6
- norm_gain: float32 [256], replicated, may hold values from 0.1 to 1.9
- w_in: bfloat16 [256, 768], replicated, may hold values from -0.375 to 0.375
- short_filter: float32 [3, 768], replicated, may hold values from -0.8 to 0.8
- long_filter: float32 [4096, 256], P('seq'), may hold values from -0.09375 to 0.09375
- medium_filter: float32 [128, 256], replicated, may hold values from -0.5 to 0.5
- skip_gain: float32 [256], replicated, may hold values from -1 to 1
- w_out: bfloat16 [256, 256], replicated, may hold values from -0.375 to 0.375
Outputs:
- result: bfloat16 [8192, 256], P(('groups', 'seq')), parts along dimension 0
The draws below stay inside these ranges and needn't reach their ends.
There are 2 independent parts, one for each index of `groups`. The reference program is written for one: setup_inputs(seed, part) draws one part's arguments, and reference() takes and returns one part's arrays. A program takes and returns all parts, laid end to end along the dimension named above; an argument that names none is the same for every part. Nothing has to cross between parts.
All inputs are finite; a program needn't handle non-finite values.
Results may differ from the reference program's by a relative error of at most 0.015.
Values may be sent and summed in bfloat16 or wider, within the bound.
A program may use at most 64 MiB of HBM per device.

```python
import jax
import jax.numpy as jnp
from jax import lax

D = 256
TAPS = 3
MED = 128
TOKENS = 4096


def block_levels(own_key, shape, cuts, low, largest):
    def one(position, parts):
        heights = jax.random.uniform(jax.random.fold_in(jax.random.fold_in(own_key, 6), position), (parts,), jnp.float32, low / len(cuts), largest / len(cuts))
        return jnp.repeat(jnp.exp(heights), shape[position] // parts).reshape((-1,) + (1,) * (len(shape) - position - 1))

    gain = one(*cuts[0])
    for cut in cuts[1:]:
        gain = gain * one(*cut)
    return gain


def bell_draw(key, shape, scale, bound, pieces=(), held_as=jnp.bfloat16):
    array = scale * jax.random.normal(key, shape, jnp.float32)
    if pieces:
        array = array * block_levels(key, shape, pieces, -0.22, 0.18)
    return jnp.clip(array, -bound, bound).astype(held_as)


def setup_inputs(seed: int = 0, part: int = 0) -> dict:
    streams_of = jax.random.split(jax.random.key(seed), 9)
    own_keys = jax.random.split(jax.random.fold_in(streams_of[8], part), 9)
    tokens = bell_draw(own_keys[0], (TOKENS, D), 1.0, 6.0, ((0, 16),))
    norm_gain = jnp.clip(1.0 + 0.18 * jax.random.normal(streams_of[1], (D,), jnp.float32), 0.1, 1.9)
    w_in = bell_draw(streams_of[2], (D, 3 * D), D ** -0.5, 0.375)
    short_filter = jnp.clip(jax.random.uniform(streams_of[3], (TAPS, 3 * D), jnp.float32, -0.8, 0.8), -0.8, 0.8)
    long_filter = bell_draw(streams_of[4], (TOKENS, D), TOKENS ** -0.5, 0.09375, ((0, 16),), jnp.float32)
    medium_filter = bell_draw(streams_of[5], (MED, D), MED ** -0.5, 0.5, (), jnp.float32)
    skip_gain = jnp.clip(jax.random.uniform(streams_of[6], (D,), jnp.float32, -1.0, 1.0), -1.0, 1.0)
    w_out = bell_draw(streams_of[7], (D, D), D ** -0.5, 0.375)
    return {"tokens": tokens, "norm_gain": norm_gain, "w_in": w_in, "short_filter": short_filter, "long_filter": long_filter, "medium_filter": medium_filter, "skip_gain": skip_gain, "w_out": w_out}


epsilon = 1e-06

def reference(tokens, norm_gain, w_in, short_filter, long_filter, medium_filter, skip_gain, w_out):
    inputs = tokens.astype(jnp.float32)
    mean_sq = lax.optimization_barrier(jnp.mean(inputs * inputs, axis=-1, keepdims=True))
    normed = (inputs * lax.rsqrt(mean_sq + epsilon) * norm_gain).astype(jnp.bfloat16)
    projected = jnp.dot(normed, w_in, preferred_element_type=jnp.float32).astype(jnp.bfloat16)
    projected = lax.optimization_barrier(projected).astype(jnp.float32)
    taps_count = short_filter.shape[0]
    padded = jnp.pad(projected, ((taps_count - 1, 0), (0, 0)))
    short_mix = jnp.zeros_like(projected)
    for tap_num in range(taps_count):
        begin = taps_count - 1 - tap_num
        short_mix = short_mix + short_filter[tap_num] * padded[begin:begin + TOKENS]
    query_part = short_mix[:, 0:D]
    key_part = short_mix[:, D:2 * D]
    value_part = short_mix[:, 2 * D:3 * D]
    signal = key_part * value_part
    fft_len = 2 * TOKENS
    spectrum = jnp.fft.rfft(signal, n=fft_len, axis=0) * jnp.fft.rfft(long_filter, n=fft_len, axis=0)
    conv_out = jnp.fft.irfft(spectrum, n=fft_len, axis=0)[:TOKENS].astype(signal.dtype)
    med_pad = jnp.pad(signal, ((MED - 1, 0), (0, 0)))

    def add_tap(tap_num, acc):
        weights = lax.dynamic_slice_in_dim(medium_filter, tap_num, 1, 0)
        window = lax.dynamic_slice_in_dim(med_pad, (MED - 1 - tap_num).astype(jnp.int32), TOKENS, 0)
        return acc + weights * window
    med_out = lax.fori_loop(0, MED, add_tap, jnp.zeros_like(signal))
    mixed_out = (query_part * (conv_out + med_out + skip_gain * signal)).astype(jnp.bfloat16)
    return jnp.dot(mixed_out, w_out, preferred_element_type=jnp.float32).astype(jnp.bfloat16)
```

```python
import math

import jax
import jax.numpy as jnp
import numpy as np
from jax import lax
from jax.sharding import PartitionSpec as P

epsilon = 1e-06
bf16 = jnp.bfloat16
f32 = jnp.float32


def tables(devices, tok_rows, chans):
    full = devices * tok_rows
    idx = np.arange(devices)
    angle = 2.0 * math.pi * ((idx[:, None] * (4 * idx[None, :] + 1)) % (4 * devices)) / (4 * devices)
    eye = np.eye(chans)
    outer_cos = np.kron(np.cos(angle), eye)
    outer_sin = np.kron(np.sin(angle), eye)
    first = np.concatenate([outer_cos.T, -outer_sin.T], axis=0)
    last = np.concatenate([outer_cos, -outer_sin], axis=1) / full
    pos = np.arange(tok_rows)
    turn = 2.0 * math.pi * ((4 * idx[:, None] + 1) * pos[None, :]) / (4 * full)
    tw_cos = np.repeat(np.cos(turn), chans, axis=0)
    tw_sin = np.repeat(np.sin(turn), chans, axis=0)
    inner = 2.0 * math.pi * (pos[:, None] * pos[None, :] % tok_rows) / tok_rows
    cos_t, sin_t = np.cos(inner), np.sin(inner)
    middle = np.block([[cos_t, -sin_t], [sin_t, cos_t]])
    return (
        first.astype(bf16),
        middle.astype(bf16),
        last.astype(bf16),
        tw_cos.astype(np.float32),
        tw_sin.astype(np.float32),
    )


def dot(a, b):
    return jnp.dot(a, b, preferred_element_type=f32)


def forward(rows, first, middle, tw_cos, tw_sin):
    half = rows.shape[0]
    part = dot(first, rows)
    re, im = part[:half], part[half:]
    turned = jnp.concatenate([re * tw_cos + im * tw_sin, im * tw_cos - re * tw_sin], axis=1)
    return dot(turned.astype(bf16), middle)


def convolve(sig, fil, first, middle, last, tw_cos, tw_sin):
    width = sig.shape[1]
    spec = forward(sig, first, middle, tw_cos, tw_sin)
    gain = forward(fil, first, middle, tw_cos, tw_sin)
    sr, si, gr, gi = spec[:, :width], spec[:, width:], gain[:, :width], gain[:, width:]
    prod = jnp.concatenate([sr * gi + si * gr, sr * gr - si * gi], axis=1).astype(bf16)
    back = dot(prod, middle)
    im, re = back[:, :width], back[:, width:]
    turned = jnp.concatenate([re * tw_cos - im * tw_sin, re * tw_sin + im * tw_cos], axis=0)
    return dot(last, turned.astype(bf16))


def from_behind(array, axis, by):
    devices = lax.axis_size(axis)
    pairs = [(i, i + by) for i in range(devices) if 0 <= i + by < devices]
    return lax.ppermute(array, axis, pairs)


def local(tokens, norm_gain, w_in, short_filter, long_filter, medium_filter, skip_gain, w_out):
    tok_rows, chan_width = tokens.shape
    devices = lax.axis_size("seq")
    my_index = lax.axis_index("seq")
    chans = chan_width // devices
    consts = [jnp.asarray(t) for t in tables(devices, tok_rows, chans)]
    med = jnp.pad(medium_filter, ((0, tok_rows - medium_filter.shape[0]), (0, 0)))
    med = med.at[0].add(skip_gain)
    taps = (long_filter + jnp.where(my_index == 0, med, 0.0)).astype(bf16)
    inputs = tokens.astype(f32)
    mean_sq = jnp.mean(inputs * inputs, axis=-1, keepdims=True)
    normed = (inputs * lax.rsqrt(mean_sq + epsilon) * norm_gain).astype(bf16)
    projected = dot(normed, w_in).astype(bf16)
    taps_count = short_filter.shape[0]
    rim_rows = from_behind(projected[tok_rows - (taps_count - 1) :], "seq", 1)
    extended = jnp.concatenate([rim_rows, projected], axis=0)
    short_mix = jnp.zeros((tok_rows, projected.shape[1]), f32)
    for tap_num in range(taps_count):
        begin = taps_count - 1 - tap_num
        short_mix = short_mix + short_filter[tap_num] * extended[begin : begin + tok_rows]
    query_part = short_mix[:, 0:chan_width]
    signal = short_mix[:, chan_width : 2 * chan_width] * short_mix[:, 2 * chan_width :]

    def spread(array):
        split = array.astype(bf16).T.reshape(devices, chans, tok_rows)
        return lax.all_to_all(split, "seq", 0, 0, tiled=True).reshape(chan_width, tok_rows)

    mixed = convolve(spread(signal), spread(taps), *consts)
    back = spread_back(mixed, devices, chans)
    mixed_out = (query_part * back.T.astype(f32)).astype(bf16)
    return dot(mixed_out, w_out).astype(bf16)


def spread_back(mixed, devices, chans):
    split = mixed.astype(bf16).reshape(devices, chans, mixed.shape[1])
    return lax.all_to_all(split, "seq", 0, 0, tiled=True).reshape(mixed.shape)


def solution(mesh):
    placed = (P(("groups", "seq"), None), P(), P(), P(), P("seq", None), P(), P(), P())
    return jax.shard_map(
        local, mesh=mesh, in_specs=placed, out_specs=P(("groups", "seq"), None), check_vma=False
    )
```

```python
import functools
import math

import jax
import jax.numpy as jnp
import numpy as np
from jax import lax
from jax.experimental import pallas as pl
from jax.experimental.pallas import tpu as pltpu
from jax.sharding import PartitionSpec as P

epsilon = 1e-06
bf16 = jnp.bfloat16
f32 = jnp.float32


def tables(devices, tok_rows, chans):
    full = devices * tok_rows
    idx = np.arange(devices)
    angle = 2.0 * math.pi * ((idx[:, None] * (4 * idx[None, :] + 1)) % (4 * devices)) / (4 * devices)
    eye = np.eye(chans)
    outer_cos = np.kron(np.cos(angle), eye)
    outer_sin = np.kron(np.sin(angle), eye)
    first = np.concatenate([outer_cos.T, -outer_sin.T], axis=0)
    last = np.concatenate([outer_cos, -outer_sin], axis=1) / full
    pos = np.arange(tok_rows)
    turn = 2.0 * math.pi * ((4 * idx[:, None] + 1) * pos[None, :]) / (4 * full)
    tw_cos = np.repeat(np.cos(turn), chans, axis=0)
    tw_sin = np.repeat(np.sin(turn), chans, axis=0)
    inner = 2.0 * math.pi * (pos[:, None] * pos[None, :] % tok_rows) / tok_rows
    cos_t, sin_t = np.cos(inner), np.sin(inner)
    middle = np.block([[cos_t, -sin_t], [sin_t, cos_t]])
    return (
        first.astype(bf16),
        middle.astype(bf16),
        last.astype(bf16),
        tw_cos.astype(np.float32),
        tw_sin.astype(np.float32),
    )


def dot(a, b):
    return jnp.dot(a, b, preferred_element_type=f32)


def forward(rows, first, middle, tw_cos, tw_sin):
    half = rows.shape[0]
    part = dot(first, rows)
    re, im = part[:half], part[half:]
    turned = jnp.concatenate([re * tw_cos + im * tw_sin, im * tw_cos - re * tw_sin], axis=1)
    return dot(turned.astype(bf16), middle)


def convolve(sig, fil, first, middle, last, tw_cos, tw_sin):
    width = sig.shape[1]
    spec = forward(sig, first, middle, tw_cos, tw_sin)
    gain = forward(fil, first, middle, tw_cos, tw_sin)
    sr, si, gr, gi = spec[:, :width], spec[:, width:], gain[:, :width], gain[:, width:]
    prod = jnp.concatenate([sr * gi + si * gr, sr * gr - si * gi], axis=1).astype(bf16)
    back = dot(prod, middle)
    im, re = back[:, :width], back[:, width:]
    turned = jnp.concatenate([re * tw_cos - im * tw_sin, re * tw_sin + im * tw_cos], axis=0)
    return dot(last, turned.astype(bf16))


def from_behind(array, axis, by):
    devices = lax.axis_size(axis)
    pairs = [(i, i + by) for i in range(devices) if 0 <= i + by < devices]
    return lax.ppermute(array, axis, pairs)


def local(tokens, norm_gain, w_in, short_filter, long_filter, medium_filter, skip_gain, w_out):
    tok_rows, chan_width = tokens.shape
    devices = lax.axis_size("seq")
    my_index = lax.axis_index("seq")
    chans = chan_width // devices
    consts = [jnp.asarray(t) for t in tables(devices, tok_rows, chans)]
    med = jnp.pad(medium_filter, ((0, tok_rows - medium_filter.shape[0]), (0, 0)))
    med = med.at[0].add(skip_gain)
    taps = (long_filter + jnp.where(my_index == 0, med, 0.0)).astype(bf16)
    inputs = tokens.astype(f32)
    mean_sq = jnp.mean(inputs * inputs, axis=-1, keepdims=True)
    normed = (inputs * lax.rsqrt(mean_sq + epsilon) * norm_gain).astype(bf16)
    projected = dot(normed, w_in).astype(bf16)
    taps_count = short_filter.shape[0]
    rim_rows = from_behind(projected[tok_rows - (taps_count - 1) :], "seq", 1)
    extended = jnp.concatenate([rim_rows, projected], axis=0)
    short_mix = jnp.zeros((tok_rows, projected.shape[1]), f32)
    for tap_num in range(taps_count):
        begin = taps_count - 1 - tap_num
        short_mix = short_mix + short_filter[tap_num] * extended[begin : begin + tok_rows]
    query_part = short_mix[:, 0:chan_width]
    signal = short_mix[:, chan_width : 2 * chan_width] * short_mix[:, 2 * chan_width :]

    def spread(array):
        split = array.astype(bf16).T.reshape(devices, chans, tok_rows)
        return lax.all_to_all(split, "seq", 0, 0, tiled=True).reshape(chan_width, tok_rows)

    mixed = convolve(spread(signal), spread(taps), *consts)
    back = spread_back(mixed, devices, chans)
    mixed_out = (query_part * back.T.astype(f32)).astype(bf16)
    return dot(mixed_out, w_out).astype(bf16)


def spread_back(mixed, devices, chans):
    split = mixed.astype(bf16).reshape(devices, chans, mixed.shape[1])
    return lax.all_to_all(split, "seq", 0, 0, tiled=True).reshape(mixed.shape)


def far_first(devices):
    return sorted(range(1, devices), key=lambda off: (abs(off - devices // 2), off))


def rms_normed(rows, gain):
    rows = rows.astype(f32)
    mean_sq = jnp.mean(rows * rows, axis=-1, keepdims=True)
    return (rows * lax.rsqrt(mean_sq + epsilon) * gain).astype(bf16)


def kernel(
    devices,
    tokens_hbm,
    gain_ref,
    w_in_hbm,
    short_ref,
    long_hbm,
    med_hbm,
    skip_ref,
    w_out_hbm,
    first_hbm,
    middle_hbm,
    last_hbm,
    tw_cos_hbm,
    tw_sin_hbm,
    out_ref,
    tokens,
    w_in,
    long_taps,
    med,
    w_out,
    first,
    middle,
    last,
    tw_cos,
    tw_sin,
    halo,
    extended,
    sends,
    arrivals,
    local_sem,
    halo_sem,
    send_sem,
    recv_sem,
):
    me = lax.axis_index("seq")
    rows, width = tokens.shape
    offsets = far_first(devices)
    rim = halo.shape[0]
    loads = [
        pltpu.make_async_copy(source, target, local_sem.at[num])
        for num, (source, target) in enumerate(
            [
                (long_hbm, long_taps),
                (med_hbm, med),
                (tokens_hbm, tokens),
                (w_in_hbm, w_in),
                (first_hbm, first),
                (tw_cos_hbm, tw_cos),
                (tw_sin_hbm, tw_sin),
                (middle_hbm, middle),
                (last_hbm, last),
                (w_out_hbm, w_out),
            ]
        )
    ]
    for load in loads:
        load.start()
    barrier = pltpu.get_barrier_semaphore()
    for off in offsets:
        pl.semaphore_signal(
            barrier,
            inc=1,
            device_id={"seq": lax.rem(me + off, devices)},
            device_id_type=pl.DeviceIdType.MESH,
        )

    def exchange(phase):
        copies = []
        for off in offsets:
            peer = lax.rem(me + off, devices)
            copy = pltpu.make_async_remote_copy(
                src_ref=sends.at[phase, peer],
                dst_ref=arrivals.at[phase, me],
                send_sem=send_sem.at[phase, off],
                recv_sem=recv_sem.at[phase, off],
                device_id={"seq": peer},
                device_id_type=pl.DeviceIdType.MESH,
            )
            copy.start()
            copies.append(copy)
        arrivals[phase, me] = sends[phase, me]
        return copies

    def arrived(phase, copies):
        for copy in copies:
            copy.wait_recv()
        return arrivals[phase].reshape(width, rows)

    loads[0].wait()
    loads[1].wait()

    @pl.when(me == 0)
    def _():
        long_taps[0 : med.shape[0], :] += med[...]
        long_taps[0:1, :] += skip_ref[...]

    sends[0] = long_taps[...].T.astype(bf16).reshape(sends.shape[1:])
    loads[2].wait()
    pl.semaphore_wait(barrier, devices - 1)
    halo_copy = pltpu.make_async_remote_copy(
        src_ref=tokens.at[pl.ds(rows - rim, rim)],
        dst_ref=halo,
        send_sem=halo_sem.at[0],
        recv_sem=halo_sem.at[1],
        device_id={"seq": lax.rem(me + 1, devices)},
        device_id_type=pl.DeviceIdType.MESH,
    )

    @pl.when(me < devices - 1)
    def _():
        halo_copy.start()

    filter_copies = exchange(0)
    normed = rms_normed(tokens[...], gain_ref[...])
    loads[3].wait()
    extended[rim:, width:] = dot(normed, w_in[:, width:]).astype(bf16).astype(f32)

    @pl.when(me == 0)
    def _():
        extended[0:rim, :] = jnp.zeros((rim, 3 * width), f32)

    @pl.when(me > 0)
    def _():
        halo_copy.wait_recv()
        extended[0:rim, :] = dot(rms_normed(halo[...], gain_ref[...]), w_in[...]).astype(bf16).astype(f32)

    def mix(part):
        lanes = pl.ds(part * width, width)
        total = short_ref[0:1, lanes] * extended[rim : rim + rows, lanes]
        for tap in range(1, short_ref.shape[0]):
            total = total + short_ref[tap : tap + 1, lanes] * extended[rim - tap : rim - tap + rows, lanes]
        return total

    sends[1] = (mix(1) * mix(2)).T.astype(bf16).reshape(sends.shape[1:])
    signal_copies = exchange(1)

    extended[rim:, :width] = dot(normed, w_in[:, :width]).astype(bf16).astype(f32)
    query = mix(0).T
    for load in loads[4:]:
        load.wait()

    def spectrum(block):
        part = dot(first[...], block)
        re, im = part[:width], part[width:]
        turned_re = (re * tw_cos[...] + im * tw_sin[...]).astype(bf16)
        turned_im = (im * tw_cos[...] - re * tw_sin[...]).astype(bf16)
        spec = dot(turned_re, middle[:rows]) + dot(turned_im, middle[rows:])
        return spec[:, :rows], spec[:, rows:]

    gr, gi = spectrum(arrived(0, filter_copies))
    sr, si = spectrum(arrived(1, signal_copies))
    back = dot((sr * gi + si * gr).astype(bf16), middle[:rows]) + dot(
        (sr * gr - si * gi).astype(bf16), middle[rows:]
    )
    im, re = back[:, :rows], back[:, rows:]
    mixed = dot(last[:, :width], (re * tw_cos[...] - im * tw_sin[...]).astype(bf16)) + dot(
        last[:, width:], (re * tw_sin[...] + im * tw_cos[...]).astype(bf16)
    )
    sends[2] = mixed.astype(bf16).reshape(sends.shape[1:])
    result_copies = exchange(2)
    gated = (query * arrived(2, result_copies).astype(f32)).T.astype(bf16)
    out_ref[...] = dot(gated, w_out[...]).astype(bf16)

    @pl.when(me < devices - 1)
    def _():
        halo_copy.wait_send()

    for copy in filter_copies + signal_copies + result_copies:
        copy.wait_send()


def fused(tokens, norm_gain, w_in, short_filter, long_filter, medium_filter, skip_gain, w_out):
    rows, width = tokens.shape
    devices = lax.axis_size("seq")
    chans = width // devices
    consts = [jnp.asarray(t) for t in tables(devices, rows, chans)]
    rim = 16
    whole = pl.BlockSpec(memory_space=pltpu.VMEM)
    far = pl.BlockSpec(memory_space=pl.ANY)
    held = [tokens, w_in, long_filter, medium_filter, w_out] + consts
    return pl.pallas_call(
        functools.partial(kernel, devices),
        out_shape=jax.ShapeDtypeStruct((rows, width), bf16),
        in_specs=[far, whole, far, whole, far, far, whole, far] + [far] * len(consts),
        out_specs=whole,
        scratch_shapes=[pltpu.VMEM(a.shape, a.dtype) for a in held]
        + [
            pltpu.VMEM((rim, width), bf16),
            pltpu.VMEM((rim + rows, 3 * width), f32),
            pltpu.VMEM((3, devices, chans, rows), bf16),
            pltpu.VMEM((3, devices, chans, rows), bf16),
            pltpu.SemaphoreType.DMA((len(held),)),
            pltpu.SemaphoreType.DMA((2,)),
            pltpu.SemaphoreType.DMA((3, devices)),
            pltpu.SemaphoreType.DMA((3, devices)),
        ],
        compiler_params=pltpu.CompilerParams(collective_id=0, has_side_effects=True),
    )(
        tokens,
        norm_gain.reshape(1, width),
        w_in,
        short_filter,
        long_filter,
        medium_filter,
        skip_gain.reshape(1, width),
        w_out,
        *consts,
    )


def solution(mesh):
    placed = (P(("groups", "seq"), None), P(), P(), P(), P("seq", None), P(), P(), P())

    def step(tokens, norm_gain, w_in, short_filter, long_filter, medium_filter, skip_gain, w_out):
        chans = tokens.shape[1] // mesh.shape["seq"]
        body = fused if chans % 16 == 0 else local
        return body(tokens, norm_gain, w_in, short_filter, long_filter, medium_filter, skip_gain, w_out)

    return jax.shard_map(
        step, mesh=mesh, in_specs=placed, out_specs=P(("groups", "seq"), None), check_vma=False
    )
```

```python
import functools
import math

import jax
import jax.numpy as jnp
import numpy as np
from jax import lax
from jax.experimental import pallas as pl
from jax.experimental.pallas import tpu as pltpu
from jax.sharding import PartitionSpec as P

epsilon = 1e-06
bf16 = jnp.bfloat16
f32 = jnp.float32


def tables(devices, tok_rows, chans):
    full = devices * tok_rows
    idx = np.arange(devices)
    angle = 2.0 * math.pi * ((idx[:, None] * (4 * idx[None, :] + 1)) % (4 * devices)) / (4 * devices)
    eye = np.eye(chans)
    outer_cos = np.kron(np.cos(angle), eye)
    outer_sin = np.kron(np.sin(angle), eye)
    first = np.concatenate([outer_cos.T, -outer_sin.T], axis=0)
    last = np.concatenate([outer_cos, -outer_sin], axis=1) / full
    pos = np.arange(tok_rows)
    turn = 2.0 * math.pi * ((4 * idx[:, None] + 1) * pos[None, :]) / (4 * full)
    tw_cos = np.repeat(np.cos(turn), chans, axis=0)
    tw_sin = np.repeat(np.sin(turn), chans, axis=0)
    inner = 2.0 * math.pi * (pos[:, None] * pos[None, :] % tok_rows) / tok_rows
    cos_t, sin_t = np.cos(inner), np.sin(inner)
    middle = np.block([[cos_t, -sin_t], [sin_t, cos_t]])
    return (
        first.astype(bf16),
        middle.astype(bf16),
        last.astype(bf16),
        tw_cos.astype(np.float32),
        tw_sin.astype(np.float32),
    )


def dot(a, b):
    return jnp.dot(a, b, preferred_element_type=f32)


def forward(rows, first, middle, tw_cos, tw_sin):
    half = rows.shape[0]
    part = dot(first, rows)
    re, im = part[:half], part[half:]
    turned = jnp.concatenate([re * tw_cos + im * tw_sin, im * tw_cos - re * tw_sin], axis=1)
    return dot(turned.astype(bf16), middle)


def convolve(sig, fil, first, middle, last, tw_cos, tw_sin):
    width = sig.shape[1]
    spec = forward(sig, first, middle, tw_cos, tw_sin)
    gain = forward(fil, first, middle, tw_cos, tw_sin)
    sr, si, gr, gi = spec[:, :width], spec[:, width:], gain[:, :width], gain[:, width:]
    prod = jnp.concatenate([sr * gi + si * gr, sr * gr - si * gi], axis=1).astype(bf16)
    back = dot(prod, middle)
    im, re = back[:, :width], back[:, width:]
    turned = jnp.concatenate([re * tw_cos - im * tw_sin, re * tw_sin + im * tw_cos], axis=0)
    return dot(last, turned.astype(bf16))


def from_behind(array, axis, by):
    devices = lax.axis_size(axis)
    pairs = [(i, i + by) for i in range(devices) if 0 <= i + by < devices]
    return lax.ppermute(array, axis, pairs)


def local(tokens, norm_gain, w_in, short_filter, long_filter, medium_filter, skip_gain, w_out):
    tok_rows, chan_width = tokens.shape
    devices = lax.axis_size("seq")
    my_index = lax.axis_index("seq")
    chans = chan_width // devices
    consts = [jnp.asarray(t) for t in tables(devices, tok_rows, chans)]
    med = jnp.pad(medium_filter, ((0, tok_rows - medium_filter.shape[0]), (0, 0)))
    med = med.at[0].add(skip_gain)
    taps = (long_filter + jnp.where(my_index == 0, med, 0.0)).astype(bf16)
    inputs = tokens.astype(f32)
    mean_sq = jnp.mean(inputs * inputs, axis=-1, keepdims=True)
    normed = (inputs * lax.rsqrt(mean_sq + epsilon) * norm_gain).astype(bf16)
    projected = dot(normed, w_in).astype(bf16)
    taps_count = short_filter.shape[0]
    rim_rows = from_behind(projected[tok_rows - (taps_count - 1) :], "seq", 1)
    extended = jnp.concatenate([rim_rows, projected], axis=0)
    short_mix = jnp.zeros((tok_rows, projected.shape[1]), f32)
    for tap_num in range(taps_count):
        begin = taps_count - 1 - tap_num
        short_mix = short_mix + short_filter[tap_num] * extended[begin : begin + tok_rows]
    query_part = short_mix[:, 0:chan_width]
    signal = short_mix[:, chan_width : 2 * chan_width] * short_mix[:, 2 * chan_width :]

    def spread(array):
        split = array.astype(bf16).T.reshape(devices, chans, tok_rows)
        return lax.all_to_all(split, "seq", 0, 0, tiled=True).reshape(chan_width, tok_rows)

    mixed = convolve(spread(signal), spread(taps), *consts)
    back = spread_back(mixed, devices, chans)
    mixed_out = (query_part * back.T.astype(f32)).astype(bf16)
    return dot(mixed_out, w_out).astype(bf16)


def spread_back(mixed, devices, chans):
    split = mixed.astype(bf16).reshape(devices, chans, mixed.shape[1])
    return lax.all_to_all(split, "seq", 0, 0, tiled=True).reshape(mixed.shape)


def rms_normed(rows, gain):
    rows = rows.astype(f32)
    mean_sq = jnp.mean(rows * rows, axis=-1, keepdims=True)
    return (rows * lax.rsqrt(mean_sq + epsilon) * gain).astype(bf16)


def kernel(
    devices,
    tokens_hbm,
    gain_hbm,
    w_in_hbm,
    short_hbm,
    long_hbm,
    med_hbm,
    skip_hbm,
    w_out_hbm,
    first_hbm,
    middle_hbm,
    last_hbm,
    tw_cos_hbm,
    tw_sin_hbm,
    out_ref,
    tokens,
    gain_ref,
    w_in,
    short_ref,
    long_taps,
    med,
    skip_ref,
    w_out,
    first,
    middle,
    last,
    tw_cos,
    tw_sin,
    halo,
    extended,
    signal,
    sends,
    arrivals,
    local_sem,
    halo_sem,
    send_sem,
    recv_sem,
):
    me = lax.axis_index("seq")
    rows, width = tokens.shape
    offsets = range(1, devices)
    rim = halo.shape[0]
    barrier = pltpu.get_barrier_semaphore()
    for off in offsets:
        pl.semaphore_signal(
            barrier,
            inc=1,
            device_id={"seq": lax.rem(me + off, devices)},
            device_id_type=pl.DeviceIdType.MESH,
        )
    loads = [
        pltpu.make_async_copy(source, target, local_sem.at[num])
        for num, (source, target) in enumerate(
            [
                (tokens_hbm, tokens),
                (gain_hbm, gain_ref),
                (w_in_hbm, w_in),
                (short_hbm, short_ref),
                (long_hbm, long_taps),
                (med_hbm, med),
                (skip_hbm, skip_ref),
                (first_hbm, first),
                (tw_cos_hbm, tw_cos),
                (tw_sin_hbm, tw_sin),
                (middle_hbm, middle),
                (last_hbm, last),
                (w_out_hbm, w_out),
            ]
        )
    ]
    for load in loads:
        load.start()

    def exchange(phase):
        copies = []
        for off in offsets:
            peer = lax.rem(me + off, devices)
            copy = pltpu.make_async_remote_copy(
                src_ref=sends.at[phase, peer],
                dst_ref=arrivals.at[phase, me],
                send_sem=send_sem.at[phase, off],
                recv_sem=recv_sem.at[phase, off],
                device_id={"seq": peer},
                device_id_type=pl.DeviceIdType.MESH,
            )
            copy.start()
            copies.append(copy)
        arrivals[phase, me] = sends[phase, me]
        return copies

    def arrived(phase, copies):
        for copy in copies:
            copy.wait_recv()
        return arrivals[phase].reshape(width, rows)

    def project(part_normed, begin):
        return dot(part_normed, w_in[:, begin:]).astype(bf16).astype(f32)

    def mix(part, begin, count):
        lanes = pl.ds(part * width, width)
        total = short_ref[0:1, lanes] * extended[rim + begin : rim + begin + count, lanes]
        for tap in range(1, short_ref.shape[0]):
            start = rim + begin - tap
            total = total + short_ref[tap : tap + 1, lanes] * extended[start : start + count, lanes]
        return total

    def turn_signal(begin, count):
        block = signal[begin : begin + count, :].T.astype(bf16)
        sends[1, :, :, begin : begin + count] = block.reshape(devices, width // devices, count)

    for load in loads[:3]:
        load.wait()
    normed = rms_normed(tokens[...], gain_ref[...])
    extended[rim:, width:] = project(normed, width)
    extended[0:rim, :] = jnp.zeros((rim, 3 * width), f32)
    for load in loads[3:7]:
        load.wait()

    @pl.when(me == 0)
    def _():
        long_taps[0 : med.shape[0], :] += med[...]
        long_taps[0:1, :] += skip_ref[...]

    sends[0] = long_taps[...].T.astype(bf16).reshape(sends.shape[1:])
    signal[...] = mix(1, 0, rows) * mix(2, 0, rows)
    turn_signal(rows // 2, rows // 2)
    pl.semaphore_wait(barrier, devices - 1)
    halo_copy = pltpu.make_async_remote_copy(
        src_ref=tokens.at[pl.ds(rows - rim, rim)],
        dst_ref=halo,
        send_sem=halo_sem.at[0],
        recv_sem=halo_sem.at[1],
        device_id={"seq": lax.rem(me + 1, devices)},
        device_id_type=pl.DeviceIdType.MESH,
    )

    @pl.when(me < devices - 1)
    def _():
        halo_copy.start()

    filter_copies = exchange(0)

    @pl.when(me > 0)
    def _():
        halo_copy.wait_recv()
        extended[0:rim, :] = project(rms_normed(halo[...], gain_ref[...]), 0)
        signal[0:rim, :] = mix(1, 0, rim) * mix(2, 0, rim)

    turn_signal(0, rows // 2)
    signal_copies = exchange(1)

    extended[rim:, :width] = dot(normed, w_in[:, :width]).astype(bf16).astype(f32)
    query = mix(0, 0, rows).T
    for load in loads[7:]:
        load.wait()

    def spectrum(block):
        part = dot(first[...], block)
        re, im = part[:width], part[width:]
        turned_re = (re * tw_cos[...] + im * tw_sin[...]).astype(bf16)
        turned_im = (im * tw_cos[...] - re * tw_sin[...]).astype(bf16)
        spec = dot(turned_re, middle[:rows]) + dot(turned_im, middle[rows:])
        return spec[:, :rows], spec[:, rows:]

    gr, gi = spectrum(arrived(0, filter_copies))
    sr, si = spectrum(arrived(1, signal_copies))
    back = dot((sr * gi + si * gr).astype(bf16), middle[:rows]) + dot(
        (sr * gr - si * gi).astype(bf16), middle[rows:]
    )
    im, re = back[:, :rows], back[:, rows:]
    mixed = dot(last[:, :width], (re * tw_cos[...] - im * tw_sin[...]).astype(bf16)) + dot(
        last[:, width:], (re * tw_sin[...] + im * tw_cos[...]).astype(bf16)
    )
    sends[2] = mixed.astype(bf16).reshape(sends.shape[1:])
    result_copies = exchange(2)
    gated = (query * arrived(2, result_copies).astype(f32)).T.astype(bf16)
    out_ref[...] = dot(gated, w_out[...]).astype(bf16)

    @pl.when(me < devices - 1)
    def _():
        halo_copy.wait_send()

    for copy in filter_copies + signal_copies + result_copies:
        copy.wait_send()


def fused(tokens, norm_gain, w_in, short_filter, long_filter, medium_filter, skip_gain, w_out):
    rows, width = tokens.shape
    devices = lax.axis_size("seq")
    chans = width // devices
    consts = [jnp.asarray(t) for t in tables(devices, rows, chans)]
    rim = 16
    held = [
        tokens,
        norm_gain.reshape(1, width),
        w_in,
        short_filter,
        long_filter,
        medium_filter,
        skip_gain.reshape(1, width),
        w_out,
        *consts,
    ]
    return pl.pallas_call(
        functools.partial(kernel, devices),
        out_shape=pltpu.VMEM((rows, width), bf16),
        in_specs=[pl.BlockSpec(memory_space=pl.ANY)] * len(held),
        out_specs=pl.BlockSpec(memory_space=pltpu.VMEM),
        scratch_shapes=[pltpu.VMEM(a.shape, a.dtype) for a in held]
        + [
            pltpu.VMEM((rim, width), bf16),
            pltpu.VMEM((rim + rows, 3 * width), f32),
            pltpu.VMEM((rows, width), f32),
            pltpu.VMEM((3, devices, chans, rows), bf16),
            pltpu.VMEM((3, devices, chans, rows), bf16),
            pltpu.SemaphoreType.DMA((len(held),)),
            pltpu.SemaphoreType.DMA((2,)),
            pltpu.SemaphoreType.DMA((3, devices)),
            pltpu.SemaphoreType.DMA((3, devices)),
        ],
        compiler_params=pltpu.CompilerParams(collective_id=0, has_side_effects=True),
    )(*held)


def solution(mesh):
    placed = (P(("groups", "seq"), None), P(), P(), P(), P("seq", None), P(), P(), P())

    def step(tokens, norm_gain, w_in, short_filter, long_filter, medium_filter, skip_gain, w_out):
        chans = tokens.shape[1] // mesh.shape["seq"]
        body = fused if chans % 16 == 0 else local
        return body(tokens, norm_gain, w_in, short_filter, long_filter, medium_filter, skip_gain, w_out)

    return jax.shard_map(
        step, mesh=mesh, in_specs=placed, out_specs=P(("groups", "seq"), None), check_vma=False
    )
```

```python
import functools
import math

import jax
import jax.numpy as jnp
import numpy as np
from jax import lax
from jax.experimental import pallas as pl
from jax.experimental.pallas import tpu as pltpu
from jax.sharding import PartitionSpec as P

epsilon = 1e-06
bf16 = jnp.bfloat16
f32 = jnp.float32


def tables(devices, tok_rows, chans):
    full = devices * tok_rows
    idx = np.arange(devices)
    angle = 2.0 * math.pi * ((idx[:, None] * (4 * idx[None, :] + 1)) % (4 * devices)) / (4 * devices)
    eye = np.eye(chans)
    outer_cos = np.kron(np.cos(angle), eye)
    outer_sin = np.kron(np.sin(angle), eye)
    first = np.concatenate([outer_cos.T, -outer_sin.T], axis=0)
    last = np.concatenate([outer_cos, -outer_sin], axis=1) / full
    pos = np.arange(tok_rows)
    turn = 2.0 * math.pi * ((4 * idx[:, None] + 1) * pos[None, :]) / (4 * full)
    tw_cos = np.repeat(np.cos(turn), chans, axis=0)
    tw_sin = np.repeat(np.sin(turn), chans, axis=0)
    inner = 2.0 * math.pi * (pos[:, None] * pos[None, :] % tok_rows) / tok_rows
    cos_t, sin_t = np.cos(inner), np.sin(inner)
    middle = np.block([[cos_t, -sin_t], [sin_t, cos_t]])
    return (
        first.astype(bf16),
        middle.astype(bf16),
        last.astype(bf16),
        tw_cos.astype(np.float32),
        tw_sin.astype(np.float32),
    )


def dot(a, b):
    return jnp.dot(a, b, preferred_element_type=f32)


def forward(rows, first, middle, tw_cos, tw_sin):
    half = rows.shape[0]
    part = dot(first, rows)
    re, im = part[:half], part[half:]
    turned = jnp.concatenate([re * tw_cos + im * tw_sin, im * tw_cos - re * tw_sin], axis=1)
    return dot(turned.astype(bf16), middle)


def convolve(sig, fil, first, middle, last, tw_cos, tw_sin):
    width = sig.shape[1]
    spec = forward(sig, first, middle, tw_cos, tw_sin)
    gain = forward(fil, first, middle, tw_cos, tw_sin)
    sr, si, gr, gi = spec[:, :width], spec[:, width:], gain[:, :width], gain[:, width:]
    prod = jnp.concatenate([sr * gi + si * gr, sr * gr - si * gi], axis=1).astype(bf16)
    back = dot(prod, middle)
    im, re = back[:, :width], back[:, width:]
    turned = jnp.concatenate([re * tw_cos - im * tw_sin, re * tw_sin + im * tw_cos], axis=0)
    return dot(last, turned.astype(bf16))


def from_behind(array, axis, by):
    devices = lax.axis_size(axis)
    pairs = [(i, i + by) for i in range(devices) if 0 <= i + by < devices]
    return lax.ppermute(array, axis, pairs)


def local(tokens, norm_gain, w_in, short_filter, long_filter, medium_filter, skip_gain, w_out):
    tok_rows, chan_width = tokens.shape
    devices = lax.axis_size("seq")
    my_index = lax.axis_index("seq")
    chans = chan_width // devices
    consts = [jnp.asarray(t) for t in tables(devices, tok_rows, chans)]
    med = jnp.pad(medium_filter, ((0, tok_rows - medium_filter.shape[0]), (0, 0)))
    med = med.at[0].add(skip_gain)
    taps = (long_filter + jnp.where(my_index == 0, med, 0.0)).astype(bf16)
    inputs = tokens.astype(f32)
    mean_sq = jnp.mean(inputs * inputs, axis=-1, keepdims=True)
    normed = (inputs * lax.rsqrt(mean_sq + epsilon) * norm_gain).astype(bf16)
    projected = dot(normed, w_in).astype(bf16)
    taps_count = short_filter.shape[0]
    rim_rows = from_behind(projected[tok_rows - (taps_count - 1) :], "seq", 1)
    extended = jnp.concatenate([rim_rows, projected], axis=0)
    short_mix = jnp.zeros((tok_rows, projected.shape[1]), f32)
    for tap_num in range(taps_count):
        begin = taps_count - 1 - tap_num
        short_mix = short_mix + short_filter[tap_num] * extended[begin : begin + tok_rows]
    query_part = short_mix[:, 0:chan_width]
    signal = short_mix[:, chan_width : 2 * chan_width] * short_mix[:, 2 * chan_width :]

    def spread(array):
        split = array.astype(bf16).T.reshape(devices, chans, tok_rows)
        return lax.all_to_all(split, "seq", 0, 0, tiled=True).reshape(chan_width, tok_rows)

    mixed = convolve(spread(signal), spread(taps), *consts)
    back = spread_back(mixed, devices, chans)
    mixed_out = (query_part * back.T.astype(f32)).astype(bf16)
    return dot(mixed_out, w_out).astype(bf16)


def spread_back(mixed, devices, chans):
    split = mixed.astype(bf16).reshape(devices, chans, mixed.shape[1])
    return lax.all_to_all(split, "seq", 0, 0, tiled=True).reshape(mixed.shape)


def rms_normed(rows, gain):
    rows = rows.astype(f32)
    mean_sq = jnp.mean(rows * rows, axis=-1, keepdims=True)
    return (rows * lax.rsqrt(mean_sq + epsilon) * gain).astype(bf16)


def kernel(
    devices,
    tokens_hbm,
    gain_hbm,
    w_in_hbm,
    short_hbm,
    long_hbm,
    med_hbm,
    skip_hbm,
    w_out_hbm,
    first_hbm,
    middle_hbm,
    last_hbm,
    tw_cos_hbm,
    tw_sin_hbm,
    out_ref,
    tokens,
    gain_ref,
    w_in,
    short_ref,
    long_taps,
    med,
    skip_ref,
    w_out,
    first,
    middle,
    last,
    tw_cos,
    tw_sin,
    halo,
    extended,
    signal,
    sends,
    arrivals,
    local_sem,
    halo_sem,
    send_sem,
    recv_sem,
):
    me = lax.axis_index("seq")
    rows, width = tokens.shape
    offsets = range(1, devices)
    rim = halo.shape[0]
    barrier = pltpu.get_barrier_semaphore()
    for off in offsets:
        pl.semaphore_signal(
            barrier,
            inc=1,
            device_id={"seq": lax.rem(me + off, devices)},
            device_id_type=pl.DeviceIdType.MESH,
        )
    loads = [
        pltpu.make_async_copy(source, target, local_sem.at[num])
        for num, (source, target) in enumerate(
            [
                (tokens_hbm, tokens),
                (gain_hbm, gain_ref),
                (w_in_hbm, w_in),
                (short_hbm, short_ref),
                (long_hbm, long_taps),
                (med_hbm, med),
                (skip_hbm, skip_ref),
                (first_hbm, first),
                (tw_cos_hbm, tw_cos),
                (tw_sin_hbm, tw_sin),
                (middle_hbm, middle),
                (last_hbm, last),
                (w_out_hbm, w_out),
            ]
        )
    ]
    for load in loads:
        load.start()

    def exchange(phase):
        for off in offsets:
            peer = lax.rem(me + off, devices)
            pltpu.make_async_remote_copy(
                src_ref=sends.at[phase, peer],
                dst_ref=arrivals.at[phase, me],
                send_sem=send_sem.at[phase],
                recv_sem=recv_sem.at[phase],
                device_id={"seq": peer},
                device_id_type=pl.DeviceIdType.MESH,
            ).start()
        arrivals[phase, me] = sends[phase, me]
        return pltpu.make_async_remote_copy(
            src_ref=sends.at[phase, pl.ds(0, devices - 1)],
            dst_ref=arrivals.at[phase, pl.ds(0, devices - 1)],
            send_sem=send_sem.at[phase],
            recv_sem=recv_sem.at[phase],
            device_id={"seq": lax.rem(me + 1, devices)},
            device_id_type=pl.DeviceIdType.MESH,
        )

    def arrived(phase, copies):
        copies.wait_recv()
        return arrivals[phase].reshape(width, rows)

    def project(part_normed, begin):
        return dot(part_normed, w_in[:, begin:]).astype(bf16).astype(f32)

    def mix(part, begin, count):
        lanes = pl.ds(part * width, width)
        total = short_ref[0:1, lanes] * extended[rim + begin : rim + begin + count, lanes]
        for tap in range(1, short_ref.shape[0]):
            start = rim + begin - tap
            total = total + short_ref[tap : tap + 1, lanes] * extended[start : start + count, lanes]
        return total

    def turn_signal(begin, count):
        block = signal[begin : begin + count, :].T.astype(bf16)
        sends[1, :, :, begin : begin + count] = block.reshape(devices, width // devices, count)

    for load in loads[:3]:
        load.wait()
    normed = rms_normed(tokens[...], gain_ref[...])
    extended[rim:, width:] = project(normed, width)
    extended[0:rim, :] = jnp.zeros((rim, 3 * width), f32)
    for load in loads[3:7]:
        load.wait()

    @pl.when(me == 0)
    def _():
        long_taps[0 : med.shape[0], :] += med[...]
        long_taps[0:1, :] += skip_ref[...]

    sends[0] = long_taps[...].T.astype(bf16).reshape(sends.shape[1:])
    signal[...] = mix(1, 0, rows) * mix(2, 0, rows)
    turn_signal(rows // 2, rows // 2)
    pl.semaphore_wait(barrier, devices - 1)
    halo_copy = pltpu.make_async_remote_copy(
        src_ref=tokens.at[pl.ds(rows - rim, rim)],
        dst_ref=halo,
        send_sem=halo_sem.at[0],
        recv_sem=halo_sem.at[1],
        device_id={"seq": lax.rem(me + 1, devices)},
        device_id_type=pl.DeviceIdType.MESH,
    )

    @pl.when(me < devices - 1)
    def _():
        halo_copy.start()

    filter_copies = exchange(0)

    @pl.when(me > 0)
    def _():
        halo_copy.wait_recv()
        extended[0:rim, :] = project(rms_normed(halo[...], gain_ref[...]), 0)
        signal[0:rim, :] = mix(1, 0, rim) * mix(2, 0, rim)

    turn_signal(0, rows // 2)
    signal_copies = exchange(1)

    extended[rim:, :width] = dot(normed, w_in[:, :width]).astype(bf16).astype(f32)
    query = mix(0, 0, rows).T
    for load in loads[7:]:
        load.wait()

    def spectrum(block):
        part = dot(first[...], block)
        re, im = part[:width], part[width:]
        turned_re = (re * tw_cos[...] + im * tw_sin[...]).astype(bf16)
        turned_im = (im * tw_cos[...] - re * tw_sin[...]).astype(bf16)
        spec = dot(turned_re, middle[:rows]) + dot(turned_im, middle[rows:])
        return spec[:, :rows], spec[:, rows:]

    gr, gi = spectrum(arrived(0, filter_copies))
    sr, si = spectrum(arrived(1, signal_copies))
    back = dot((sr * gi + si * gr).astype(bf16), middle[:rows]) + dot(
        (sr * gr - si * gi).astype(bf16), middle[rows:]
    )
    im, re = back[:, :rows], back[:, rows:]
    mixed = dot(last[:, :width], (re * tw_cos[...] - im * tw_sin[...]).astype(bf16)) + dot(
        last[:, width:], (re * tw_sin[...] + im * tw_cos[...]).astype(bf16)
    )
    sends[2] = mixed.astype(bf16).reshape(sends.shape[1:])
    result_copies = exchange(2)
    gated = (query * arrived(2, result_copies).astype(f32)).T.astype(bf16)
    out_ref[...] = dot(gated, w_out[...]).astype(bf16)

    @pl.when(me < devices - 1)
    def _():
        halo_copy.wait_send()

    for copies in (filter_copies, signal_copies, result_copies):
        copies.wait_send()


def fused(tokens, norm_gain, w_in, short_filter, long_filter, medium_filter, skip_gain, w_out):
    rows, width = tokens.shape
    devices = lax.axis_size("seq")
    chans = width // devices
    consts = [jnp.asarray(t) for t in tables(devices, rows, chans)]
    rim = 16
    held = [
        tokens,
        norm_gain.reshape(1, width),
        w_in,
        short_filter,
        long_filter,
        medium_filter,
        skip_gain.reshape(1, width),
        w_out,
        *consts,
    ]
    return pl.pallas_call(
        functools.partial(kernel, devices),
        out_shape=pltpu.VMEM((rows, width), bf16),
        in_specs=[pl.BlockSpec(memory_space=pl.ANY)] * len(held),
        out_specs=pl.BlockSpec(memory_space=pltpu.VMEM),
        scratch_shapes=[pltpu.VMEM(a.shape, a.dtype) for a in held]
        + [
            pltpu.VMEM((rim, width), bf16),
            pltpu.VMEM((rim + rows, 3 * width), f32),
            pltpu.VMEM((rows, width), f32),
            pltpu.VMEM((3, devices, chans, rows), bf16),
            pltpu.VMEM((3, devices, chans, rows), bf16),
            pltpu.SemaphoreType.DMA((len(held),)),
            pltpu.SemaphoreType.DMA((2,)),
            pltpu.SemaphoreType.DMA((3,)),
            pltpu.SemaphoreType.DMA((3,)),
        ],
        compiler_params=pltpu.CompilerParams(collective_id=0, has_side_effects=True),
    )(*held)


def solution(mesh):
    placed = (P(("groups", "seq"), None), P(), P(), P(), P("seq", None), P(), P(), P())

    def step(tokens, norm_gain, w_in, short_filter, long_filter, medium_filter, skip_gain, w_out):
        chans = tokens.shape[1] // mesh.shape["seq"]
        body = fused if chans % 16 == 0 else local
        return body(tokens, norm_gain, w_in, short_filter, long_filter, medium_filter, skip_gain, w_out)

    return jax.shard_map(
        step, mesh=mesh, in_specs=placed, out_specs=P(("groups", "seq"), None), check_vma=False
    )
```

```python
import functools
import math

import jax
import jax.numpy as jnp
import numpy as np
from jax import lax
from jax.experimental import pallas as pl
from jax.experimental.pallas import tpu as pltpu
from jax.sharding import PartitionSpec as P

epsilon = 1e-06
bf16 = jnp.bfloat16
f32 = jnp.float32


def tables(devices, tok_rows, chans):
    full = devices * tok_rows
    idx = np.arange(devices)
    angle = 2.0 * math.pi * ((idx[:, None] * (4 * idx[None, :] + 1)) % (4 * devices)) / (4 * devices)
    eye = np.eye(chans)
    outer_cos = np.kron(np.cos(angle), eye)
    outer_sin = np.kron(np.sin(angle), eye)
    first = np.concatenate([outer_cos.T, -outer_sin.T], axis=0)
    last = np.concatenate([outer_cos, -outer_sin], axis=1) / full
    pos = np.arange(tok_rows)
    turn = 2.0 * math.pi * ((4 * idx[:, None] + 1) * pos[None, :]) / (4 * full)
    tw_cos = np.repeat(np.cos(turn), chans, axis=0)
    tw_sin = np.repeat(np.sin(turn), chans, axis=0)
    inner = 2.0 * math.pi * (pos[:, None] * pos[None, :] % tok_rows) / tok_rows
    cos_t, sin_t = np.cos(inner), np.sin(inner)
    middle = np.block([[cos_t, -sin_t], [sin_t, cos_t]])
    return (
        first.astype(bf16),
        middle.astype(bf16),
        last.astype(bf16),
        tw_cos.astype(np.float32),
        tw_sin.astype(np.float32),
    )


def dot(a, b):
    return jnp.dot(a, b, preferred_element_type=f32)


def forward(rows, first, middle, tw_cos, tw_sin):
    half = rows.shape[0]
    part = dot(first, rows)
    re, im = part[:half], part[half:]
    turned = jnp.concatenate([re * tw_cos + im * tw_sin, im * tw_cos - re * tw_sin], axis=1)
    return dot(turned.astype(bf16), middle)


def convolve(sig, fil, first, middle, last, tw_cos, tw_sin):
    width = sig.shape[1]
    spec = forward(sig, first, middle, tw_cos, tw_sin)
    gain = forward(fil, first, middle, tw_cos, tw_sin)
    sr, si, gr, gi = spec[:, :width], spec[:, width:], gain[:, :width], gain[:, width:]
    prod = jnp.concatenate([sr * gi + si * gr, sr * gr - si * gi], axis=1).astype(bf16)
    back = dot(prod, middle)
    im, re = back[:, :width], back[:, width:]
    turned = jnp.concatenate([re * tw_cos - im * tw_sin, re * tw_sin + im * tw_cos], axis=0)
    return dot(last, turned.astype(bf16))


def from_behind(array, axis, by):
    devices = lax.axis_size(axis)
    pairs = [(i, i + by) for i in range(devices) if 0 <= i + by < devices]
    return lax.ppermute(array, axis, pairs)


def local(tokens, norm_gain, w_in, short_filter, long_filter, medium_filter, skip_gain, w_out):
    tok_rows, chan_width = tokens.shape
    devices = lax.axis_size("seq")
    my_index = lax.axis_index("seq")
    chans = chan_width // devices
    consts = [jnp.asarray(t) for t in tables(devices, tok_rows, chans)]
    med = jnp.pad(medium_filter, ((0, tok_rows - medium_filter.shape[0]), (0, 0)))
    med = med.at[0].add(skip_gain)
    taps = (long_filter + jnp.where(my_index == 0, med, 0.0)).astype(bf16)
    inputs = tokens.astype(f32)
    mean_sq = jnp.mean(inputs * inputs, axis=-1, keepdims=True)
    normed = (inputs * lax.rsqrt(mean_sq + epsilon) * norm_gain).astype(bf16)
    projected = dot(normed, w_in).astype(bf16)
    taps_count = short_filter.shape[0]
    rim_rows = from_behind(projected[tok_rows - (taps_count - 1) :], "seq", 1)
    extended = jnp.concatenate([rim_rows, projected], axis=0)
    short_mix = jnp.zeros((tok_rows, projected.shape[1]), f32)
    for tap_num in range(taps_count):
        begin = taps_count - 1 - tap_num
        short_mix = short_mix + short_filter[tap_num] * extended[begin : begin + tok_rows]
    query_part = short_mix[:, 0:chan_width]
    signal = short_mix[:, chan_width : 2 * chan_width] * short_mix[:, 2 * chan_width :]

    def spread(array):
        split = array.astype(bf16).T.reshape(devices, chans, tok_rows)
        return lax.all_to_all(split, "seq", 0, 0, tiled=True).reshape(chan_width, tok_rows)

    mixed = convolve(spread(signal), spread(taps), *consts)
    back = spread_back(mixed, devices, chans)
    mixed_out = (query_part * back.T.astype(f32)).astype(bf16)
    return dot(mixed_out, w_out).astype(bf16)


def spread_back(mixed, devices, chans):
    split = mixed.astype(bf16).reshape(devices, chans, mixed.shape[1])
    return lax.all_to_all(split, "seq", 0, 0, tiled=True).reshape(mixed.shape)


def rms_normed(rows, gain):
    rows = rows.astype(f32)
    mean_sq = jnp.mean(rows * rows, axis=-1, keepdims=True)
    return (rows * lax.rsqrt(mean_sq + epsilon) * gain).astype(bf16)


def kernel(
    devices,
    tokens_hbm,
    gain_hbm,
    w_in_hbm,
    short_hbm,
    long_hbm,
    med_hbm,
    skip_hbm,
    w_out_hbm,
    first_hbm,
    middle_hbm,
    last_hbm,
    tw_cos_hbm,
    tw_sin_hbm,
    out_ref,
    tokens,
    gain_ref,
    w_in,
    short_ref,
    long_taps,
    med,
    skip_ref,
    w_out,
    first,
    middle,
    last,
    tw_cos,
    tw_sin,
    halo,
    extended,
    signal,
    sends,
    arrivals,
    local_sem,
    halo_sem,
    send_sem,
    recv_sem,
):
    me = lax.axis_index("seq")
    rows, width = tokens.shape
    offsets = range(1, devices)
    rim = halo.shape[0]
    barrier = pltpu.get_barrier_semaphore()
    for off in offsets:
        pl.semaphore_signal(
            barrier,
            inc=1,
            device_id={"seq": lax.rem(me + off, devices)},
            device_id_type=pl.DeviceIdType.MESH,
        )
    loads = [
        pltpu.make_async_copy(source, target, local_sem.at[num])
        for num, (source, target) in enumerate(
            [
                (tokens_hbm, tokens),
                (gain_hbm, gain_ref),
                (w_in_hbm, w_in),
                (short_hbm, short_ref),
                (long_hbm, long_taps),
                (med_hbm, med),
                (skip_hbm, skip_ref),
                (first_hbm, first),
                (tw_cos_hbm, tw_cos),
                (tw_sin_hbm, tw_sin),
                (middle_hbm, middle),
                (last_hbm, last),
                (w_out_hbm, w_out),
            ]
        )
    ]
    for load in loads:
        load.start()

    def exchange(phase):
        for off in (offsets if phase else reversed(offsets)):
            peer = lax.rem(me + off, devices)
            pltpu.make_async_remote_copy(
                src_ref=sends.at[phase, peer],
                dst_ref=arrivals.at[phase, me],
                send_sem=send_sem.at[phase],
                recv_sem=recv_sem.at[phase],
                device_id={"seq": peer},
                device_id_type=pl.DeviceIdType.MESH,
            ).start()
        arrivals[phase, me] = sends[phase, me]
        return pltpu.make_async_remote_copy(
            src_ref=sends.at[phase, pl.ds(0, devices - 1)],
            dst_ref=arrivals.at[phase, pl.ds(0, devices - 1)],
            send_sem=send_sem.at[phase],
            recv_sem=recv_sem.at[phase],
            device_id={"seq": lax.rem(me + 1, devices)},
            device_id_type=pl.DeviceIdType.MESH,
        )

    def arrived(phase, copies):
        copies.wait_recv()
        return arrivals[phase].reshape(width, rows)

    def project(part_normed, begin):
        return dot(part_normed, w_in[:, begin:]).astype(bf16).astype(f32)

    def mix(part, begin, count):
        lanes = pl.ds(part * width, width)
        total = short_ref[0:1, lanes] * extended[rim + begin : rim + begin + count, lanes]
        for tap in range(1, short_ref.shape[0]):
            start = rim + begin - tap
            total = total + short_ref[tap : tap + 1, lanes] * extended[start : start + count, lanes]
        return total

    def turn_signal(begin, count):
        block = signal[begin : begin + count, :].T.astype(bf16)
        sends[1, :, :, begin : begin + count] = block.reshape(devices, width // devices, count)

    for load in loads[:3]:
        load.wait()
    normed = rms_normed(tokens[...], gain_ref[...])
    extended[rim:, width:] = project(normed, width)
    extended[0:rim, :] = jnp.zeros((rim, 3 * width), f32)
    for load in loads[3:7]:
        load.wait()

    @pl.when(me == 0)
    def _():
        long_taps[0 : med.shape[0], :] += med[...]
        long_taps[0:1, :] += skip_ref[...]

    sends[0] = long_taps[...].T.astype(bf16).reshape(sends.shape[1:])
    signal[...] = mix(1, 0, rows) * mix(2, 0, rows)
    turn_signal(rows // 2, rows // 2)
    pl.semaphore_wait(barrier, devices - 1)
    halo_copy = pltpu.make_async_remote_copy(
        src_ref=tokens.at[pl.ds(rows - rim, rim)],
        dst_ref=halo,
        send_sem=halo_sem.at[0],
        recv_sem=halo_sem.at[1],
        device_id={"seq": lax.rem(me + 1, devices)},
        device_id_type=pl.DeviceIdType.MESH,
    )

    @pl.when(me < devices - 1)
    def _():
        halo_copy.start()

    filter_copies = exchange(0)

    @pl.when(me > 0)
    def _():
        halo_copy.wait_recv()
        extended[0:rim, :] = project(rms_normed(halo[...], gain_ref[...]), 0)
        signal[0:rim, :] = mix(1, 0, rim) * mix(2, 0, rim)

    turn_signal(0, rows // 2)
    signal_copies = exchange(1)

    extended[rim:, :width] = dot(normed, w_in[:, :width]).astype(bf16).astype(f32)
    query = mix(0, 0, rows).T
    for load in loads[7:]:
        load.wait()

    def spectrum(block):
        part = dot(first[...], block)
        re, im = part[:width], part[width:]
        turned = jnp.concatenate(
            [re * tw_cos[...] + im * tw_sin[...], im * tw_cos[...] - re * tw_sin[...]], axis=1
        )
        spec = dot(turned.astype(bf16), middle[...])
        return spec[:, :rows], spec[:, rows:]

    gr, gi = spectrum(arrived(0, filter_copies))
    sr, si = spectrum(arrived(1, signal_copies))
    prod = jnp.concatenate([sr * gi + si * gr, sr * gr - si * gi], axis=1)
    back = dot(prod.astype(bf16), middle[...])
    im, re = back[:, :rows], back[:, rows:]
    turned = jnp.concatenate(
        [re * tw_cos[...] - im * tw_sin[...], re * tw_sin[...] + im * tw_cos[...]], axis=0
    )
    mixed = dot(last[...], turned.astype(bf16))
    sends[2] = mixed.astype(bf16).reshape(sends.shape[1:])
    result_copies = exchange(2)
    gated = (query * arrived(2, result_copies).astype(f32)).astype(bf16).T
    out_ref[...] = dot(gated, w_out[...]).astype(bf16)

    @pl.when(me < devices - 1)
    def _():
        halo_copy.wait_send()

    for copies in (filter_copies, signal_copies, result_copies):
        copies.wait_send()


def fused(tokens, norm_gain, w_in, short_filter, long_filter, medium_filter, skip_gain, w_out):
    rows, width = tokens.shape
    devices = lax.axis_size("seq")
    chans = width // devices
    consts = [jnp.asarray(t) for t in tables(devices, rows, chans)]
    rim = 16
    held = [
        tokens,
        norm_gain.reshape(1, width),
        w_in,
        short_filter,
        long_filter,
        medium_filter,
        skip_gain.reshape(1, width),
        w_out,
        *consts,
    ]
    return pl.pallas_call(
        functools.partial(kernel, devices),
        out_shape=pltpu.VMEM((rows, width), bf16),
        in_specs=[pl.BlockSpec(memory_space=pl.ANY)] * len(held),
        out_specs=pl.BlockSpec(memory_space=pltpu.VMEM),
        scratch_shapes=[pltpu.VMEM(a.shape, a.dtype) for a in held]
        + [
            pltpu.VMEM((rim, width), bf16),
            pltpu.VMEM((rim + rows, 3 * width), f32),
            pltpu.VMEM((rows, width), f32),
            pltpu.VMEM((3, devices, chans, rows), bf16),
            pltpu.VMEM((3, devices, chans, rows), bf16),
            pltpu.SemaphoreType.DMA((len(held),)),
            pltpu.SemaphoreType.DMA((2,)),
            pltpu.SemaphoreType.DMA((3,)),
            pltpu.SemaphoreType.DMA((3,)),
        ],
        compiler_params=pltpu.CompilerParams(collective_id=0, has_side_effects=True),
    )(*held)


def solution(mesh):
    placed = (P(("groups", "seq"), None), P(), P(), P(), P("seq", None), P(), P(), P())

    def step(tokens, norm_gain, w_in, short_filter, long_filter, medium_filter, skip_gain, w_out):
        chans = tokens.shape[1] // mesh.shape["seq"]
        body = fused if chans % 16 == 0 else local
        return body(tokens, norm_gain, w_in, short_filter, long_filter, medium_filter, skip_gain, w_out)

    return jax.shard_map(
        step, mesh=mesh, in_specs=placed, out_specs=P(("groups", "seq"), None), check_vma=False
    )
```
